128 devices in a mesh: patch: 16 (over x, y_hi, core), head: 8 (over y_lo, z).
Axes of the slice: x: 4, y: 4 (y_hi: 2, y_lo: 2; y = y_hi * 2 + y_lo), z: 4, core: 2. Of those that a mesh axis runs over, the one named last changes fastest.
Arguments:
- image_query: bfloat16 [16384, 2048], P(('patch', 'head')), may hold values from -120 to 120
- image_key: bfloat16 [16384, 2048], P(('patch', 'head')), may hold values from -6 to 6
- image_value: bfloat16 [16384, 2048], P(('patch', 'head')), may hold values from -6 to 6
- positions: int32 [3, 16384], P(None, ('patch', 'head')), may hold values from 0 to 63
- stale_key: bfloat16 [16384, 2048], P('patch', 'head'), may hold values from -6 to 6
- stale_value: bfloat16 [16384, 2048], P('patch', 'head'), may hold values from -6 to 6
- text_query: bfloat16 [256, 2048], P(None, 'head'), may hold values from -120 to 120
- text_key: bfloat16 [256, 2048], P(None, 'head'), may hold values from -6 to 6
- text_value: bfloat16 [256, 2048], P(None, 'head'), may hold values from -6 to 6
- text_len: int32 [1], replicated, may hold values from 64 to 256
Outputs:
- image_out: bfloat16 [16384, 2048], P(('patch', 'head'))
- text_out: bfloat16 [256, 2048], P(None, 'head')
The draws below stay inside these ranges and needn't reach their ends.
All inputs are finite; a program needn't handle non-finite values.
Results may differ from the reference program's by a relative error of at most 0.0086.
Values may be sent and summed in bfloat16 or wider, within the bound.
A program may use at most 128 MiB of HBM per device.

```python
import jax
import jax.numpy as jnp
import numpy as np
from jax import lax

H = 16
HD = 128
TXT = 256
P_SIZE = 1024
S = 16384
N_PATCH = 16


def shared_image(key):
    return jnp.clip(jax.random.normal(jax.random.fold_in(key, 100), (S, H * HD), jnp.float32), -6.0, 6.0)


def shared_text(key):
    return jnp.clip(jax.random.normal(jax.random.fold_in(key, 200), (TXT, H * HD), jnp.float32), -6.0, 6.0)


def drawn(key, base):
    return 3.0 * jnp.clip(jax.random.normal(key, base.shape, jnp.float32), -6.0, 6.0)


def draw_image_key(key, part):
    base = shared_image(key)
    return base.astype(jnp.bfloat16)


def draw_image_query(key, part):
    base = shared_image(key)
    key = jax.random.fold_in(key, 2)
    return drawn(key, base).astype(jnp.bfloat16)


def draw_text_key(key, part):
    base = shared_text(key)
    return base.astype(jnp.bfloat16)


def draw_text_query(key, part):
    base = shared_text(key)
    key = jax.random.fold_in(key, 4)
    return drawn(key, base).astype(jnp.bfloat16)


def plant(values, own_key, smallest, largest):
    index_at = [jax.random.randint(jax.random.fold_in(own_key, axis), (), 0, length) for axis, length in enumerate(values.shape)]
    main_axis = values.shape.index(max(values.shape))
    beside = index_at[:main_axis] + [(index_at[main_axis] + 1) % values.shape[main_axis]] + index_at[main_axis + 1:]
    return values.at[tuple(index_at)].set(smallest).at[tuple(beside)].set(largest)


def level_of(stream_key, shape, split, low, high):
    def one(dim, blocks):
        steps = jax.random.uniform(jax.random.fold_in(jax.random.fold_in(stream_key, 6), dim), (blocks,), jnp.float32, low / len(split), high / len(split))
        return jnp.repeat(jnp.exp(steps), shape[dim] // blocks).reshape((-1,) + (1,) * (len(shape) - dim - 1))

    gain = one(*split[0])
    for cut in split[1:]:
        gain = gain * one(*cut)
    return gain


def normal_values(own_key, extent, scale, most, cuts=(), kind=jnp.bfloat16):
    gain = level_of(own_key, extent, cuts, -0.22, 0.18) if cuts else 1.0
    values = jax.random.normal(own_key, extent, jnp.float32) * scale * gain
    return jnp.minimum(jnp.maximum(values, -most), most).astype(kind)


def setup_inputs(seed: int = 0) -> dict:
    seeds = jax.random.split(jax.random.key(seed), 11)
    image_query = draw_image_query(jax.random.fold_in(seeds[10], 71), 0)
    image_key = draw_image_key(jax.random.fold_in(seeds[10], 71), 0)
    image_value = normal_values(seeds[2], (S, H * HD), 1.0, 6.0, ((0, 128),))
    positions = plant(jax.random.randint(seeds[3], (3, S), 0, 64), jax.random.fold_in(seeds[3], 1), 0, 63).astype(jnp.int32)
    stale_key = normal_values(seeds[4], (S, H * HD), 1.0, 6.0, ((0, 16), (1, 8)))
    stale_value = normal_values(seeds[5], (S, H * HD), 1.0, 6.0, ((0, 16), (1, 8)))
    text_query = draw_text_query(jax.random.fold_in(seeds[10], 71), 0)
    text_key = draw_text_key(jax.random.fold_in(seeds[10], 71), 0)
    text_value = normal_values(seeds[8], (TXT, H * HD), 1.0, 6.0, ((1, 8),))
    text_len = jax.random.randint(seeds[9], (1,), TXT // 4, TXT + 1).astype(jnp.int32)
    return {"image_query": image_query, "image_key": image_key, "image_value": image_value, "positions": positions, "stale_key": stale_key, "stale_value": stale_value, "text_query": text_query, "text_key": text_key, "text_value": text_value, "text_len": text_len}


THETA = 256.0


def pair_tables(head_dim):
    first = head_dim // 8
    second = (head_dim - first) // 2
    parts = [first, second, head_dim - first - second]
    freqs = []
    which = []
    for axis_id in range(3):
        width = parts[axis_id]
        for index in range(width // 2):
            freqs.append(THETA ** (-2.0 * index / width))
            which.append(axis_id)
    return np.array(freqs, dtype=np.float32), np.array(which, dtype=np.int32), parts


def rotate(values, positions):
    freqs, which, parts = pair_tables(HD)
    count = values.shape[0]
    pos = positions.astype(jnp.float32)
    angles = jnp.take(pos, jnp.asarray(which), axis=0).T * jnp.asarray(freqs)[None, :]
    cosine = jnp.cos(angles)[:, None, :]
    sine = jnp.sin(angles)[:, None, :]
    heads = values.astype(jnp.float32).reshape(count, -1, HD)
    pieces = []
    begin = 0
    pair_start = 0
    for width in parts:
        half = width // 2
        low = heads[:, :, begin:begin + half]
        high = heads[:, :, begin + half:begin + width]
        c = cosine[:, :, pair_start:pair_start + half]
        s = sine[:, :, pair_start:pair_start + half]
        pieces.append(low * c - high * s)
        pieces.append(low * s + high * c)
        begin = begin + width
        pair_start = pair_start + half
    return jnp.concatenate(pieces, axis=2).reshape(count, -1).astype(jnp.bfloat16)


def split_heads(values):
    return values.reshape(values.shape[0], H, HD).transpose(1, 0, 2)


def attend(queries, keys, values, valid):
    scale = HD ** -0.5

    def one_head(args):
        query, key, value = args
        scores = jnp.dot(query, key.T, preferred_element_type=jnp.float32) * scale
        scores = jnp.where(valid[None, :], scores, -jnp.inf)
        top = jnp.max(scores, axis=1, keepdims=True)
        weights = jnp.exp(scores - top)
        total = jnp.sum(weights, axis=1, keepdims=True)
        mixed = jnp.dot(weights.astype(jnp.bfloat16), value, preferred_element_type=jnp.float32)
        return mixed / total

    result = lax.map(one_head, (split_heads(queries), split_heads(keys), split_heads(values)))
    return result.transpose(1, 0, 2).reshape(queries.shape[0], H * HD).astype(jnp.bfloat16)


def reference(image_query, image_key, image_value, positions, stale_key, stale_value, text_query, text_key, text_value, text_len):
    rotated_query = rotate(image_query, positions)
    rotated_key = rotate(image_key, positions)
    text_valid = jnp.arange(TXT) < text_len[0]
    valid = jnp.concatenate([jnp.ones((S,), bool), text_valid])
    zero = jnp.zeros((), jnp.int32)

    def one_patch(index):
        start = (index * P_SIZE).astype(jnp.int32)
        keys = lax.dynamic_update_slice(stale_key, lax.dynamic_slice_in_dim(rotated_key, start, P_SIZE, 0), (start, zero))
        values = lax.dynamic_update_slice(stale_value, lax.dynamic_slice_in_dim(image_value, start, P_SIZE, 0), (start, zero))
        keys = jnp.concatenate([keys, text_key], axis=0)
        values = jnp.concatenate([values, text_value], axis=0)
        queries = lax.dynamic_slice_in_dim(rotated_query, start, P_SIZE, 0)
        return attend(queries, keys, values, valid)

    image_out = lax.map(one_patch, jnp.arange(N_PATCH, dtype=jnp.int32)).reshape(S, H * HD)
    text_out = attend(text_query, jnp.concatenate([rotated_key, text_key], axis=0), jnp.concatenate([image_value, text_value], axis=0), valid)
    return image_out, text_out
```

```python
import functools

import jax
import jax.numpy as jnp
import numpy as np
from jax import lax
from jax.experimental import pallas as pl
from jax.experimental.pallas import tpu as pltpu
from jax.sharding import PartitionSpec as P

HD = 128
THETA = 256.0
MESH = pl.DeviceIdType.MESH
SCALE = 1.4426950408889634 * HD ** (-0.5)
LOW = -1e30
TILE = 1024
PIECE = 512
BLOCK = 128
TXT = 256

NEAR_A, NEAR_B, FAR, OWN = (4, 6, 8, 10), (5, 7, 9, 11), (12, 13, 14, 15), (0, 1, 2, 3)
ITEMS = [
    (0, NEAR_A), (1, NEAR_A),
    (0, (16, 17, 2, 3)), (1, (0, 1, 18, 19)),
    (0, NEAR_B), (1, NEAR_B),
    (2, OWN), (3, OWN),
    (2, NEAR_A), (3, NEAR_A),
    (2, NEAR_B), (3, NEAR_B),
    (2, FAR), (3, FAR),
    (0, FAR), (1, FAR),
]


def rotation_tables():
    first = HD // 8
    second = (HD - first) // 2
    freqs = np.zeros((HD,), np.float32)
    which = np.zeros((HD,), np.int32)
    swap = np.zeros((HD, HD), np.float32)
    begin = 0
    for axis_id, width in enumerate([first, second, HD - first - second]):
        half = width // 2
        for index in range(half):
            low, high = begin + index, begin + index + half
            freqs[low] = freqs[high] = np.float32(THETA ** (-2.0 * index / width))
            which[low] = which[high] = axis_id
            swap[high, low] = -1.0
            swap[low, high] = 1.0
        begin += width
    return freqs, which, swap


def pick(i, values):
    out = values[0]
    for j in range(1, len(values)):
        if values[j] != values[j - 1]:
            out = jnp.where(i >= j, values[j], out)
    return out


def split_scaled(x):
    f = x.astype(jnp.float32) * SCALE
    hi = f.astype(jnp.bfloat16)
    lo = (f - hi.astype(jnp.float32)).astype(jnp.bfloat16)
    return jnp.concatenate([hi, lo], axis=1)


def scores(qq, k):
    return lax.dot_general(
        qq, jnp.concatenate([k, k], axis=1), (((1,), (1,)), ((), ())), preferred_element_type=jnp.float32
    )


def fold(s, v, m, a):
    top = jnp.maximum(m, jnp.max(s, axis=1, keepdims=True))
    p = jnp.exp2(s - top).astype(jnp.bfloat16)
    vv = jnp.concatenate([v, jnp.ones_like(v)], axis=1)
    a = a * jnp.exp2(m - top) + jnp.dot(p, vv, preferred_element_type=jnp.float32)
    return top, a


def kernel(
    q_ref, k_ref, v_ref, cos_ref, sin_ref, swap_ref, sk_ref, sv_ref, tq_ref, tk_ref, tv_ref, len_ref,
    out_ref, tout_ref,
    qh, kvh, qb, qq_s, kv, m_s, acc_s, o_send, l_send, o_recv, l_recv, out_stage, t_send, t_recv, t_stage,
    q_sem, kv_sem, near_sem, core_sem, far_sem, y_sem, o_sem, out_sem, t_sem, tg_sem,
):
    p = lax.axis_index("patch")
    h = lax.axis_index("head")
    x, y, c = p // 4, (p // 2) % 2, p % 2
    me = h * 2 + c
    rank = x * 2 + y

    def at(x_, y_, c_):
        return (x_ * 4 + y_ * 2 + c_, h)

    left, right = (x + 3) % 4, (x + 1) % 4
    lanes = pl.ds(pl.multiple_of(c * HD, HD), HD)

    barrier = pltpu.get_barrier_semaphore()

    def greet_plane(d, _):
        to = (me + d) % 16
        pl.semaphore_signal(barrier, inc=1, device_id=(x * 4 + y * 2 + to % 2, to // 2), device_id_type=MESH)
        return 0

    def greet_patch(d, _):
        to = (p + d) % 16
        pl.semaphore_signal(barrier, inc=1, device_id=(to, h), device_id_type=MESH)
        return 0

    lax.fori_loop(1, 16, greet_plane, 0)
    lax.fori_loop(1, 16, greet_patch, 0)
    pl.semaphore_wait(barrier, 30)

    def remote(src, dst, sems, index, to):
        return pltpu.make_async_remote_copy(
            src_ref=src, dst_ref=dst, send_sem=sems.at[(0,) + index], recv_sem=sems.at[(1,) + index],
            device_id=to, device_id_type=MESH,
        )

    def near(half, side, core, part):
        src = (sk_ref, sv_ref)[part].at[pl.ds(half * PIECE, PIECE), pl.ds(core * HD, HD)]
        piece = 4 + 4 * side + 2 * c + half
        return remote(src, kv.at[piece, part], near_sem, (side, c, half, part, core), at((right, left)[side], y, core))

    def near_arrives(half, side, core, part):
        piece = 4 + 4 * side + 2 * core + half
        ref = kv.at[piece, part]
        return remote(ref, ref, near_sem, (side, core, half, part, c), at(right, y, c))

    def near_each(half, fn):
        for side in range(2):
            for part in range(2):
                for core in range(2):
                    fn(half, side, core, part)

    near_each(0, lambda *a: near(*a).start())
    near_each(1, lambda *a: near(*a).start())

    other = pl.ds(pl.multiple_of((1 - c) * HD, HD), HD)

    def across(half, part):
        src = (sk_ref, sv_ref)[part].at[pl.ds(half * PIECE, PIECE), other]
        return remote(src, kv.at[2 * c + half, part], core_sem, (half, part), at(x, y, 1 - c))

    def across_arrives(half, part):
        ref = kv.at[2 * (1 - c) + half, part]
        return remote(ref, ref, core_sem, (half, part), at(x, y, 1 - c))

    cosine, sine, swap = cos_ref[...], sin_ref[...], swap_ref[...]

    def rotated(ref, g):
        value = ref[:, g * HD : (g + 1) * HD]
        turned = jnp.dot(value, swap, preferred_element_type=jnp.float32)
        return (value.astype(jnp.float32) * cosine + turned * sine).astype(jnp.bfloat16)

    def q_copy(d):
        to = (me + d) % 16
        return remote(qh.at[to], qb.at[c, h], q_sem, (d,), (x * 4 + y * 2 + to % 2, to // 2))

    def q_arrives(d):
        fr = (me + 16 - d) % 16
        ref = qb.at[fr % 2, fr // 2]
        return remote(ref, ref, q_sem, (d,), (x * 4 + y * 2 + fr % 2, fr // 2))

    def fresh_at(core, head):
        return kv.at[16 + 2 * core + head // 4, :, pl.ds(pl.multiple_of((head % 4) * BLOCK, BLOCK), BLOCK), :]

    def kv_copy(d):
        to = (me + d) % 16
        return remote(kvh.at[to], fresh_at(c, h), kv_sem, (d,), (x * 4 + y * 2 + to % 2, to // 2))

    def kv_arrives(d):
        fr = (me + 16 - d) % 16
        ref = fresh_at(fr % 2, fr // 2)
        return remote(ref, ref, kv_sem, (d,), (x * 4 + y * 2 + fr % 2, fr // 2))

    def loop(low, high, fn):
        def step(d, _):
            fn(d)
            return 0

        lax.fori_loop(low, high, step, 0)

    for g in range(16):
        qh[g] = rotated(q_ref, g)
    loop(1, 16, lambda d: q_copy(d).start())
    for g in range(16):
        kvh[g, 0] = rotated(k_ref, g)
        kvh[g, 1] = v_ref[:, g * HD : (g + 1) * HD]
    loop(1, 16, lambda d: kv_copy(d).start())
    for half in range(2):
        for part in range(2):
            across(half, part).start()

    for half in range(2):
        kv[2 * c + half, 0] = sk_ref[half * PIECE : (half + 1) * PIECE, lanes]
        kv[2 * c + half, 1] = sv_ref[half * PIECE : (half + 1) * PIECE, lanes]
    qb[c, h] = qh[me]
    row = pl.multiple_of((h % 4) * BLOCK, BLOCK)
    kv[16 + 2 * c + h // 4, :, pl.ds(row, BLOCK), :] = kvh[me]

    def clear(t):
        m_s[t] = jnp.full((TILE, HD), LOW, jnp.float32)
        acc_s[t] = jnp.zeros((TILE, 2 * HD), jnp.float32)

    loop(0, 4, clear)

    def ready(t):
        qq_s[t] = split_scaled(qb[t].reshape(TILE, HD))

    def y_copy(t):
        return remote(qb.at[t], qb.at[2 + t], y_sem, (t,), at(x, 1 - y, c))

    def y_arrives(t):
        return remote(qb.at[2 + t], qb.at[2 + t], y_sem, (t,), at(x, 1 - y, c))

    loop(1, 16, lambda d: q_arrives(d).wait_recv())
    for t in range(2):
        y_copy(t).start()
    loop(0, 2, ready)

    def far(half, core, part):
        src = kv.at[4 + 4 * part + 2 * core + half, part]
        dst = kv.at[12 + 2 * core + half, part]
        return remote(src, dst, far_sem, (core, half, part), at((right, left)[part], y, c))

    def far_arrives(half, core, part):
        ref = kv.at[12 + 2 * core + half, part]
        return remote(ref, ref, far_sem, (core, half, part), at(right, y, c))

    def near_ready(half):
        near_each(half, lambda *a: near_arrives(*a).wait_recv())
        for core in range(2):
            for part in range(2):
                far(half, core, part).start()

    valid = lax.broadcasted_iota(jnp.int32, (1, TXT), 1) < len_ref[0]

    def text_keys(t):
        s = jnp.where(valid, scores(qq_s[t], tk_ref[:, lanes]), LOW)
        m, a = fold(s, tv_ref[:, lanes], m_s[t][:, :1], acc_s[t])
        m_s[t] = jnp.broadcast_to(m, (TILE, HD))
        acc_s[t] = a

    def text_copy(d):
        to = (rank + d) % 8
        src = t_send.at[:, pl.ds(pl.multiple_of(to * 32, 32), 32), :]
        return remote(src, t_recv.at[rank], t_sem, (d,), at(to // 2, to % 2, c))

    def text_arrives(d):
        fr = (rank + 8 - d) % 8
        return remote(t_recv.at[fr], t_recv.at[fr], t_sem, (d,), at(fr // 2, fr % 2, c))

    def text_queries():
        qq = split_scaled(tq_ref[:, lanes])
        m = jnp.full((TXT, 1), LOW, jnp.float32)
        a = jnp.zeros((TXT, 2 * HD), jnp.float32)
        for piece in range(16, 20):
            m, a = fold(scores(qq, kv[piece, 0]), kv[piece, 1], m, a)
        here = valid & (rank == 0)
        s = jnp.where(here, scores(qq, tk_ref[:, lanes]), LOW)
        m, a = fold(s, tv_ref[:, lanes], m, a)
        total = a[:, HD:]
        t_send[0] = a[:, :HD] / total
        t_send[1] = m + jnp.log2(total)
        loop(1, 8, lambda d: text_copy(d).start())
        t_recv[rank] = t_send[:, pl.ds(pl.multiple_of(rank * 32, 32), 32), :]

    def gather_copy(d):
        to = (p + d) % 16
        dst = tout_ref.at[pl.ds(pl.multiple_of(rank * 32, 32), 32), lanes]
        return remote(t_stage, dst, tg_sem, (d,), (to, h))

    def gather_arrives(d):
        fr = (p + 16 - d) % 16
        rows = pl.ds(pl.multiple_of((fr // 2) * 32, 32), 32)
        ref = tout_ref.at[rows, pl.ds(pl.multiple_of((fr % 2) * HD, HD), HD)]
        return remote(ref, ref, tg_sem, (d,), (fr, h))

    def text_merge():
        loop(1, 8, lambda d: text_arrives(d).wait_recv())
        top = t_recv[0, 1]
        for r in range(1, 8):
            top = jnp.maximum(top, t_recv[r, 1])
        total = jnp.zeros((32, HD), jnp.float32)
        mixed = jnp.zeros((32, HD), jnp.float32)
        for r in range(8):
            w = jnp.exp2(t_recv[r, 1] - top)
            total += w
            mixed += w * t_recv[r, 0]
        done = (mixed / total).astype(jnp.bfloat16)
        t_stage[...] = done
        loop(1, 16, lambda d: gather_copy(d).start())
        tout_ref[pl.ds(pl.multiple_of(rank * 32, 32), 32), lanes] = done

    eye = lax.broadcasted_iota(jnp.int32, (HD, HD), 0) == lax.broadcasted_iota(jnp.int32, (HD, HD), 1)

    def o_copy(t):
        return remote(o_send.at[t], o_recv.at[t], o_sem, (t, 0), at(x, 1 - y, c))

    def l_copy(t):
        return remote(l_send.at[t], l_recv.at[t], o_sem, (t, 1), at(x, 1 - y, c))

    def give(t):
        total = acc_s[t][:, HD:]
        o_send[t - 2] = (acc_s[t][:, :HD] / total).astype(jnp.bfloat16)
        level = m_s[t] + jnp.log2(total)
        rows = []
        for b in range(TILE // HD):
            rows.append(jnp.sum(jnp.where(eye, level[b * HD : (b + 1) * HD], 0.0), axis=0, keepdims=True))
        l_send[t - 2] = jnp.concatenate(rows, axis=0)
        o_copy(t - 2).start()
        l_copy(t - 2).start()

    def out_copy(t, d):
        to = (h + d) % 8
        cols = pl.ds(pl.multiple_of(me * HD, HD), HD)
        return remote(out_stage.at[t, to], out_ref.at[:, cols], out_sem, (t, c, d), (x * 4 + y * 2 + t, to))

    def out_arrives(core, d):
        fr = (h + 8 - d) % 8
        ref = out_ref.at[:, pl.ds(pl.multiple_of((fr * 2 + core) * HD, HD), HD)]
        return remote(ref, ref, out_sem, (c, core, d), (x * 4 + y * 2 + core, fr))

    def take(t):
        o_copy(t).wait_recv()
        l_copy(t).wait_recv()
        total = acc_s[t][:, HD:]
        mine = acc_s[t][:, :HD] / total
        level = m_s[t] + jnp.log2(total)
        theirs = o_recv[t].astype(jnp.float32)
        got = l_recv[t]
        for b in range(TILE // HD):
            block = slice(b * HD, (b + 1) * HD)
            lev = jnp.sum(jnp.where(eye, got[b : b + 1], 0.0), axis=1, keepdims=True)
            top = jnp.maximum(level[block], lev)
            wa, wb = jnp.exp2(level[block] - top), jnp.exp2(lev - top)
            out_stage[t, b] = ((mine[block] * wa + theirs[block] * wb) / (wa + wb)).astype(jnp.bfloat16)
        first = (t + 2 - c) % 2

        loop(1, 8, lambda d: out_copy(t, d).start())

        @pl.when(first == 0)
        def _():
            out_ref[:, pl.ds(pl.multiple_of(me * HD, HD), HD)] = out_stage[t, h]

        @pl.when(first != 0)
        def _():
            out_copy(t, 0).start()

    def item(i):
        @pl.when(i == 0)
        def _():
            near_ready(0)

        @pl.when(i == 2)
        def _():
            loop(1, 16, lambda d: kv_arrives(d).wait_recv())
            for half in range(2):
                for part in range(2):
                    across_arrives(half, part).wait_recv()

        @pl.when(i == 4)
        def _():
            near_ready(1)

        @pl.when(i == 6)
        def _():
            loop(0, 2, text_keys)
            text_queries()
            for t in range(2):
                y_arrives(t).wait_recv()
            loop(2, 4, ready)

        @pl.when(i == 9)
        def _():
            text_merge()

        @pl.when(i == 12)
        def _():
            for half in range(2):
                for core in range(2):
                    for part in range(2):
                        far_arrives(half, core, part).wait_recv()

        t = pick(i, [q for q, _ in ITEMS])
        ids = [pick(i, [pieces[n] for _, pieces in ITEMS]) for n in range(4)]
        qq = qq_s[t]
        m = m_s[t][:, :1]
        a = acc_s[t]
        s = scores(qq, kv[ids[0], 0])
        for n in range(4):
            following = scores(qq, kv[ids[n + 1], 0]) if n < 3 else None
            m, a = fold(s, kv[ids[n], 1], m, a)
            s = following
        m_s[t] = jnp.broadcast_to(m, (TILE, HD))
        acc_s[t] = a

        @pl.when((i >= 12) & (i < 14))
        def _():
            give(t)

        @pl.when(i >= 14)
        def _():
            take(t)

    loop(0, 16, item)

    loop(1, 16, lambda d: gather_arrives(d).wait_recv())
    loop(1, 8, lambda d: out_arrives(c, d).wait_recv())
    loop(0, 8, lambda d: out_arrives(1 - c, d).wait_recv())
    near_each(0, lambda *a: near(*a).wait_send())
    near_each(1, lambda *a: near(*a).wait_send())
    loop(1, 16, lambda d: q_copy(d).wait_send())
    loop(1, 16, lambda d: kv_copy(d).wait_send())
    for half in range(2):
        for part in range(2):
            across(half, part).wait_send()
            for core in range(2):
                far(half, core, part).wait_send()
    for t in range(2):
        y_copy(t).wait_send()
        o_copy(t).wait_send()
        l_copy(t).wait_send()
    loop(1, 8, lambda d: text_copy(d).wait_send())
    loop(1, 16, lambda d: gather_copy(d).wait_send())
    loop(1, 8, lambda d: out_copy(c, d).wait_send())
    loop(0, 8, lambda d: out_copy(1 - c, d).wait_send())


def body(image_query, image_key, image_value, positions, stale_key, stale_value, text_query, text_key, text_value, text_len):
    freqs, which, swap = rotation_tables()
    pos = positions.astype(jnp.float32)
    angles = jnp.take(pos, jnp.asarray(which), axis=0).T * jnp.asarray(freqs)[None, :]
    dma = pltpu.SemaphoreType.DMA
    bf, f32 = jnp.bfloat16, jnp.float32
    vmem = pl.BlockSpec(memory_space=pltpu.VMEM)
    return pl.pallas_call(
        kernel,
        out_shape=(
            jax.ShapeDtypeStruct(image_query.shape, bf),
            jax.ShapeDtypeStruct(text_query.shape, bf),
        ),
        in_specs=[vmem] * 11 + [pl.BlockSpec(memory_space=pltpu.SMEM)],
        out_specs=(vmem, vmem),
        scratch_shapes=[
            pltpu.VMEM((16, BLOCK, HD), bf),
            pltpu.VMEM((16, 2, BLOCK, HD), bf),
            pltpu.VMEM((4, 8, BLOCK, HD), bf),
            pltpu.VMEM((4, TILE, 2 * HD), bf),
            pltpu.VMEM((20, 2, PIECE, HD), bf),
            pltpu.VMEM((4, TILE, HD), f32),
            pltpu.VMEM((4, TILE, 2 * HD), f32),
            pltpu.VMEM((2, TILE, HD), bf),
            pltpu.VMEM((2, 8, HD), f32),
            pltpu.VMEM((2, TILE, HD), bf),
            pltpu.VMEM((2, 8, HD), f32),
            pltpu.VMEM((2, 8, BLOCK, HD), bf),
            pltpu.VMEM((2, TXT, HD), f32),
            pltpu.VMEM((8, 2, 32, HD), f32),
            pltpu.VMEM((32, HD), bf),
            dma((2, 16)),
            dma((2, 16)),
            dma((2, 2, 2, 2, 2, 2)),
            dma((2, 2, 2)),
            dma((2, 2, 2, 2)),
            dma((2, 2)),
            dma((2, 2, 2)),
            dma((2, 2, 2, 8)),
            dma((2, 8)),
            dma((2, 16)),
        ],
        compiler_params=pltpu.CompilerParams(
            collective_id=0, has_side_effects=True, vmem_limit_bytes=56 * 2**20
        ),
        name="joint_attention",
    )(
        image_query, image_key, image_value, jnp.cos(angles), jnp.sin(angles), jnp.asarray(swap, bf),
        stale_key, stale_value, text_query, text_key, text_value, text_len,
    )


def solution(mesh):
    return jax.shard_map(
        body,
        mesh=mesh,
        in_specs=(
            P(("patch", "head"), None),
            P(("patch", "head"), None),
            P(("patch", "head"), None),
            P(None, ("patch", "head")),
            P("patch", "head"),
            P("patch", "head"),
            P(None, "head"),
            P(None, "head"),
            P(None, "head"),
            P(),
        ),
        out_specs=(P(("patch", "head"), None), P(None, "head")),
        check_vma=False,
    )
```

```python
import functools

import jax
import jax.numpy as jnp
import numpy as np
from jax import lax
from jax.experimental import pallas as pl
from jax.experimental.pallas import tpu as pltpu
from jax.sharding import PartitionSpec as P

HD = 128
THETA = 256.0
MESH = pl.DeviceIdType.MESH
SCALE = 1.4426950408889634 * HD ** (-0.5)
LOW = -1e30
TILE = 1024
PIECE = 512
BLOCK = 128
TXT = 256

NEAR_A, NEAR_B, FAR, OWN = (4, 6, 8, 10), (5, 7, 9, 11), (12, 13, 14, 15), (0, 1, 2, 3)
ITEMS = [
    (0, NEAR_A), (1, NEAR_A),
    (0, (16, 17, 2, 3)), (1, (0, 1, 18, 19)),
    (0, NEAR_B), (1, NEAR_B),
    (2, OWN), (3, OWN),
    (2, NEAR_A), (3, NEAR_A),
    (2, NEAR_B), (3, NEAR_B),
    (2, FAR), (3, FAR),
    (0, FAR), (1, FAR),
]


def rotation_tables():
    first = HD // 8
    second = (HD - first) // 2
    freqs = np.zeros((3, HD), np.float32)
    swap = np.zeros((HD, HD), np.float32)
    begin = 0
    for axis_id, width in enumerate([first, second, HD - first - second]):
        half = width // 2
        for index in range(half):
            low, high = begin + index, begin + index + half
            freqs[axis_id, low] = freqs[axis_id, high] = np.float32(THETA ** (-2.0 * index / width))
            swap[high, low] = -1.0
            swap[low, high] = 1.0
        begin += width
    terms = []
    for _ in range(3):
        term = freqs.astype(jnp.bfloat16)
        terms.append(term)
        freqs = freqs - term.astype(np.float32)
    return np.concatenate(terms + [np.zeros((7, HD), jnp.bfloat16)], axis=0), swap


def pick(i, values):
    out = values[0]
    for j in range(1, len(values)):
        if values[j] != values[j - 1]:
            out = jnp.where(i >= j, values[j], out)
    return out


def split_scaled(x):
    f = x.astype(jnp.float32) * SCALE
    hi = f.astype(jnp.bfloat16)
    lo = (f - hi.astype(jnp.float32)).astype(jnp.bfloat16)
    return jnp.concatenate([hi, lo], axis=1)


def scores(qq, k):
    return lax.dot_general(
        qq, jnp.concatenate([k, k], axis=1), (((1,), (1,)), ((), ())), preferred_element_type=jnp.float32
    )


def fold(s, v, m, a):
    top = jnp.maximum(m, jnp.max(s, axis=1, keepdims=True))
    p = jnp.exp2(s - top).astype(jnp.bfloat16)
    vv = jnp.concatenate([v, jnp.ones_like(v)], axis=1)
    a = a * jnp.exp2(m - top) + jnp.dot(p, vv, preferred_element_type=jnp.float32)
    return top, a


def kernel(
    q_ref, k_ref, v_ref, pos_ref, freq_ref, swap_ref, sk_ref, sv_ref, tq_ref, tk_ref, tv_ref, len_ref,
    out_ref, tout_ref,
    qh, kvh, qb, qq_s, kv, m_s, acc_s, o_send, l_send, o_recv, l_recv, out_stage, t_send, t_recv, t_stage,
    q_sem, kv_sem, near_sem, core_sem, far_sem, y_sem, o_sem, out_sem, t_sem, tg_sem,
):
    p = lax.axis_index("patch")
    h = lax.axis_index("head")
    x, y, c = p // 4, (p // 2) % 2, p % 2
    me = h * 2 + c
    rank = x * 2 + y

    def at(x_, y_, c_):
        return (x_ * 4 + y_ * 2 + c_, h)

    left, right = (x + 3) % 4, (x + 1) % 4
    lanes = pl.ds(pl.multiple_of(c * HD, HD), HD)

    barrier = pltpu.get_barrier_semaphore()

    for d in range(1, 16):
        to = (me + d) % 16
        pl.semaphore_signal(barrier, inc=1, device_id=(x * 4 + y * 2 + to % 2, to // 2), device_id_type=MESH)
        pl.semaphore_signal(barrier, inc=1, device_id=((p + d) % 16, h), device_id_type=MESH)

    def remote(src, dst, sems, index, to):
        return pltpu.make_async_remote_copy(
            src_ref=src, dst_ref=dst, send_sem=sems.at[(0,) + index], recv_sem=sems.at[(1,) + index],
            device_id=to, device_id_type=MESH,
        )

    def near(half, side, core, part):
        src = (sk_ref, sv_ref)[part].at[pl.ds(half * PIECE, PIECE), pl.ds(core * HD, HD)]
        piece = 4 + 4 * side + 2 * c + half
        return remote(src, kv.at[piece, part], near_sem, (side, c, half, part, core), at((right, left)[side], y, core))

    def near_arrives(half, side, core, part):
        piece = 4 + 4 * side + 2 * core + half
        ref = kv.at[piece, part]
        return remote(ref, ref, near_sem, (side, core, half, part, c), at(right, y, c))

    def near_each(half, fn):
        for side in range(2):
            for part in range(2):
                for core in range(2):
                    fn(half, side, core, part)

    other = pl.ds(pl.multiple_of((1 - c) * HD, HD), HD)

    def across(half, part):
        src = (sk_ref, sv_ref)[part].at[pl.ds(half * PIECE, PIECE), other]
        return remote(src, kv.at[2 * c + half, part], core_sem, (half, part), at(x, y, 1 - c))

    def across_arrives(half, part):
        ref = kv.at[2 * (1 - c) + half, part]
        return remote(ref, ref, core_sem, (half, part), at(x, y, 1 - c))

    swap = swap_ref[...]
    pos = pos_ref[...].astype(jnp.float32)
    pos = jnp.concatenate([pos, pos, pos, jnp.zeros((7, BLOCK), jnp.float32)], axis=0).astype(jnp.bfloat16)
    angle = lax.dot_general(pos, freq_ref[...], (((0,), (0,)), ((), ())), preferred_element_type=jnp.float32)
    cosine, sine = jnp.cos(angle), jnp.sin(angle)

    def rotated(ref, g):
        value = ref[:, g * HD : (g + 1) * HD]
        turned = jnp.dot(value, swap, preferred_element_type=jnp.float32)
        return (value.astype(jnp.float32) * cosine + turned * sine).astype(jnp.bfloat16)

    def q_copy(d):
        to = (me + d) % 16
        return remote(qh.at[to], qb.at[c, h], q_sem, (d,), (x * 4 + y * 2 + to % 2, to // 2))

    def q_arrives(d):
        fr = (me + 16 - d) % 16
        ref = qb.at[fr % 2, fr // 2]
        return remote(ref, ref, q_sem, (d,), (x * 4 + y * 2 + fr % 2, fr // 2))

    def fresh_at(core, head):
        return kv.at[16 + 2 * core + head // 4, :, pl.ds(pl.multiple_of((head % 4) * BLOCK, BLOCK), BLOCK), :]

    def kv_copy(d):
        to = (me + d) % 16
        return remote(kvh.at[to], fresh_at(c, h), kv_sem, (d,), (x * 4 + y * 2 + to % 2, to // 2))

    def kv_arrives(d):
        fr = (me + 16 - d) % 16
        ref = fresh_at(fr % 2, fr // 2)
        return remote(ref, ref, kv_sem, (d,), (x * 4 + y * 2 + fr % 2, fr // 2))

    def loop(low, high, fn):
        def step(d, _):
            fn(d)
            return 0

        lax.fori_loop(low, high, step, 0)

    for g in range(16):
        qh[g] = rotated(q_ref, g)
    for g in range(16):
        kvh[g, 0] = rotated(k_ref, g)
        kvh[g, 1] = v_ref[:, g * HD : (g + 1) * HD]

    pl.semaphore_wait(barrier, 30)
    loop(1, 16, lambda d: q_copy(d).start())
    near_each(0, lambda *a: near(*a).start())
    loop(1, 16, lambda d: kv_copy(d).start())
    near_each(1, lambda *a: near(*a).start())
    for half in range(2):
        for part in range(2):
            across(half, part).start()

    for half in range(2):
        kv[2 * c + half, 0] = sk_ref[half * PIECE : (half + 1) * PIECE, lanes]
        kv[2 * c + half, 1] = sv_ref[half * PIECE : (half + 1) * PIECE, lanes]
    qb[c, h] = qh[me]
    row = pl.multiple_of((h % 4) * BLOCK, BLOCK)
    kv[16 + 2 * c + h // 4, :, pl.ds(row, BLOCK), :] = kvh[me]

    def clear(t):
        m_s[t] = jnp.full((TILE, HD), LOW, jnp.float32)
        acc_s[t] = jnp.zeros((TILE, 2 * HD), jnp.float32)

    loop(0, 4, clear)

    def ready(t):
        qq_s[t] = split_scaled(qb[t].reshape(TILE, HD))

    def y_copy(t):
        return remote(qb.at[t], qb.at[2 + t], y_sem, (t,), at(x, 1 - y, c))

    def y_arrives(t):
        return remote(qb.at[2 + t], qb.at[2 + t], y_sem, (t,), at(x, 1 - y, c))

    loop(1, 16, lambda d: q_arrives(d).wait_recv())
    for t in range(2):
        y_copy(t).start()
    loop(0, 2, ready)

    def far(half, core, part):
        src = kv.at[4 + 4 * part + 2 * core + half, part]
        dst = kv.at[12 + 2 * core + half, part]
        return remote(src, dst, far_sem, (core, half, part), at((right, left)[part], y, c))

    def far_arrives(half, core, part):
        ref = kv.at[12 + 2 * core + half, part]
        return remote(ref, ref, far_sem, (core, half, part), at(right, y, c))

    def near_ready(half):
        near_each(half, lambda *a: near_arrives(*a).wait_recv())
        for core in range(2):
            for part in range(2):
                far(half, core, part).start()

    valid = lax.broadcasted_iota(jnp.int32, (1, TXT), 1) < len_ref[0]

    def text_keys(t):
        s = jnp.where(valid, scores(qq_s[t], tk_ref[:, lanes]), LOW)
        m, a = fold(s, tv_ref[:, lanes], jnp.max(m_s[t], axis=1, keepdims=True), acc_s[t])
        m_s[t] = jnp.broadcast_to(m, (TILE, HD))
        acc_s[t] = a

    def text_copy(d):
        to = (rank + d) % 8
        src = t_send.at[:, pl.ds(pl.multiple_of(to * 32, 32), 32), :]
        return remote(src, t_recv.at[rank], t_sem, (d,), at(to // 2, to % 2, c))

    def text_arrives(d):
        fr = (rank + 8 - d) % 8
        return remote(t_recv.at[fr], t_recv.at[fr], t_sem, (d,), at(fr // 2, fr % 2, c))

    def text_queries():
        qq = split_scaled(tq_ref[:, lanes])
        m = jnp.full((TXT, 1), LOW, jnp.float32)
        a = jnp.zeros((TXT, 2 * HD), jnp.float32)
        for piece in range(16, 20):
            m, a = fold(scores(qq, kv[piece, 0]), kv[piece, 1], m, a)
        here = valid & (rank == 0)
        s = jnp.where(here, scores(qq, tk_ref[:, lanes]), LOW)
        m, a = fold(s, tv_ref[:, lanes], m, a)
        total = a[:, HD:]
        t_send[0] = a[:, :HD] / total
        t_send[1] = m + jnp.log2(total)
        loop(1, 8, lambda d: text_copy(d).start())
        t_recv[rank] = t_send[:, pl.ds(pl.multiple_of(rank * 32, 32), 32), :]

    def gather_copy(d):
        to = (p + d) % 16
        dst = tout_ref.at[pl.ds(pl.multiple_of(rank * 32, 32), 32), lanes]
        return remote(t_stage, dst, tg_sem, (d,), (to, h))

    def gather_arrives(d):
        fr = (p + 16 - d) % 16
        rows = pl.ds(pl.multiple_of((fr // 2) * 32, 32), 32)
        ref = tout_ref.at[rows, pl.ds(pl.multiple_of((fr % 2) * HD, HD), HD)]
        return remote(ref, ref, tg_sem, (d,), (fr, h))

    def text_merge():
        loop(1, 8, lambda d: text_arrives(d).wait_recv())
        top = t_recv[0, 1]
        for r in range(1, 8):
            top = jnp.maximum(top, t_recv[r, 1])
        total = jnp.zeros((32, HD), jnp.float32)
        mixed = jnp.zeros((32, HD), jnp.float32)
        for r in range(8):
            w = jnp.exp2(t_recv[r, 1] - top)
            total += w
            mixed += w * t_recv[r, 0]
        done = (mixed / total).astype(jnp.bfloat16)
        t_stage[...] = done
        loop(1, 16, lambda d: gather_copy(d).start())
        tout_ref[pl.ds(pl.multiple_of(rank * 32, 32), 32), lanes] = done

    eye = lax.broadcasted_iota(jnp.int32, (HD, HD), 0) == lax.broadcasted_iota(jnp.int32, (HD, HD), 1)

    def o_copy(t):
        return remote(o_send.at[t], o_recv.at[t], o_sem, (t, 0), at(x, 1 - y, c))

    def l_copy(t):
        return remote(l_send.at[t], l_recv.at[t], o_sem, (t, 1), at(x, 1 - y, c))

    def give(t):
        total = acc_s[t][:, HD:]
        o_send[t - 2] = (acc_s[t][:, :HD] / total).astype(jnp.bfloat16)
        level = m_s[t] + jnp.log2(total)
        rows = []
        for b in range(TILE // HD):
            rows.append(jnp.sum(jnp.where(eye, level[b * HD : (b + 1) * HD], 0.0), axis=0, keepdims=True))
        l_send[t - 2] = jnp.concatenate(rows, axis=0)
        o_copy(t - 2).start()
        l_copy(t - 2).start()

    def out_copy(t, d):
        to = (h + d) % 8
        cols = pl.ds(pl.multiple_of(me * HD, HD), HD)
        return remote(out_stage.at[t, to], out_ref.at[:, cols], out_sem, (t, c, d), (x * 4 + y * 2 + t, to))

    def out_arrives(core, d):
        fr = (h + 8 - d) % 8
        ref = out_ref.at[:, pl.ds(pl.multiple_of((fr * 2 + core) * HD, HD), HD)]
        return remote(ref, ref, out_sem, (c, core, d), (x * 4 + y * 2 + core, fr))

    def take(t):
        o_copy(t).wait_recv()
        l_copy(t).wait_recv()
        total = acc_s[t][:, HD:]
        mine = acc_s[t][:, :HD] / total
        level = m_s[t] + jnp.log2(total)
        theirs = o_recv[t].astype(jnp.float32)
        got = l_recv[t]
        for b in range(TILE // HD):
            block = slice(b * HD, (b + 1) * HD)
            lev = jnp.sum(jnp.where(eye, got[b : b + 1], 0.0), axis=1, keepdims=True)
            top = jnp.maximum(level[block], lev)
            wa, wb = jnp.exp2(level[block] - top), jnp.exp2(lev - top)
            out_stage[t, b] = ((mine[block] * wa + theirs[block] * wb) / (wa + wb)).astype(jnp.bfloat16)
        first = (t + 2 - c) % 2

        loop(1, 8, lambda d: out_copy(t, d).start())

        @pl.when(first == 0)
        def _():
            out_ref[:, pl.ds(pl.multiple_of(me * HD, HD), HD)] = out_stage[t, h]

        @pl.when(first != 0)
        def _():
            out_copy(t, 0).start()

    def item(i):
        @pl.when(i == 0)
        def _():
            near_ready(0)

        @pl.when(i == 2)
        def _():
            loop(1, 16, lambda d: kv_arrives(d).wait_recv())
            for half in range(2):
                for part in range(2):
                    across_arrives(half, part).wait_recv()

        @pl.when(i == 4)
        def _():
            near_ready(1)

        @pl.when(i == 6)
        def _():
            loop(0, 2, text_keys)
            text_queries()
            for t in range(2):
                y_arrives(t).wait_recv()
            loop(2, 4, ready)

        @pl.when(i == 9)
        def _():
            text_merge()

        @pl.when(i == 12)
        def _():
            for half in range(2):
                for core in range(2):
                    for part in range(2):
                        far_arrives(half, core, part).wait_recv()

        t = pick(i, [q for q, _ in ITEMS])
        ids = [pick(i, [pieces[n] for _, pieces in ITEMS]) for n in range(4)]
        qq = qq_s[t]
        m = jnp.max(m_s[t], axis=1, keepdims=True)
        a = acc_s[t]
        s = scores(qq, kv[ids[0], 0])
        for n in range(4):
            following = scores(qq, kv[ids[n + 1], 0]) if n < 3 else None
            m, a = fold(s, kv[ids[n], 1], m, a)
            s = following
        m_s[t] = jnp.broadcast_to(m, (TILE, HD))
        acc_s[t] = a

        @pl.when((i >= 12) & (i < 14))
        def _():
            give(t)

        @pl.when(i >= 14)
        def _():
            take(t)

    loop(0, 16, item)

    loop(1, 16, lambda d: gather_arrives(d).wait_recv())
    loop(1, 8, lambda d: out_arrives(c, d).wait_recv())
    loop(0, 8, lambda d: out_arrives(1 - c, d).wait_recv())
    near_each(0, lambda *a: near(*a).wait_send())
    near_each(1, lambda *a: near(*a).wait_send())
    loop(1, 16, lambda d: q_copy(d).wait_send())
    loop(1, 16, lambda d: kv_copy(d).wait_send())
    for half in range(2):
        for part in range(2):
            across(half, part).wait_send()
            for core in range(2):
                far(half, core, part).wait_send()
    for t in range(2):
        y_copy(t).wait_send()
        o_copy(t).wait_send()
        l_copy(t).wait_send()
    loop(1, 8, lambda d: text_copy(d).wait_send())
    loop(1, 16, lambda d: gather_copy(d).wait_send())
    loop(1, 8, lambda d: out_copy(c, d).wait_send())
    loop(0, 8, lambda d: out_copy(1 - c, d).wait_send())


def body(image_query, image_key, image_value, positions, stale_key, stale_value, text_query, text_key, text_value, text_len):
    freqs, swap = rotation_tables()
    dma = pltpu.SemaphoreType.DMA
    bf, f32 = jnp.bfloat16, jnp.float32
    vmem = pl.BlockSpec(memory_space=pltpu.VMEM)
    return pl.pallas_call(
        kernel,
        out_shape=(
            jax.ShapeDtypeStruct(image_query.shape, bf),
            jax.ShapeDtypeStruct(text_query.shape, bf),
        ),
        in_specs=[vmem] * 11 + [pl.BlockSpec(memory_space=pltpu.SMEM)],
        out_specs=(vmem, vmem),
        scratch_shapes=[
            pltpu.VMEM((16, BLOCK, HD), bf),
            pltpu.VMEM((16, 2, BLOCK, HD), bf),
            pltpu.VMEM((4, 8, BLOCK, HD), bf),
            pltpu.VMEM((4, TILE, 2 * HD), bf),
            pltpu.VMEM((20, 2, PIECE, HD), bf),
            pltpu.VMEM((4, TILE, HD), f32),
            pltpu.VMEM((4, TILE, 2 * HD), f32),
            pltpu.VMEM((2, TILE, HD), bf),
            pltpu.VMEM((2, 8, HD), f32),
            pltpu.VMEM((2, TILE, HD), bf),
            pltpu.VMEM((2, 8, HD), f32),
            pltpu.VMEM((2, 8, BLOCK, HD), bf),
            pltpu.VMEM((2, TXT, HD), f32),
            pltpu.VMEM((8, 2, 32, HD), f32),
            pltpu.VMEM((32, HD), bf),
            dma((2, 16)),
            dma((2, 16)),
            dma((2, 2, 2, 2, 2, 2)),
            dma((2, 2, 2)),
            dma((2, 2, 2, 2)),
            dma((2, 2)),
            dma((2, 2, 2)),
            dma((2, 2, 2, 8)),
            dma((2, 8)),
            dma((2, 16)),
        ],
        compiler_params=pltpu.CompilerParams(
            collective_id=0, has_side_effects=True, vmem_limit_bytes=56 * 2**20
        ),
        name="joint_attention",
    )(
        image_query, image_key, image_value, positions, jnp.asarray(freqs), jnp.asarray(swap, bf),
        stale_key, stale_value, text_query, text_key, text_value, text_len,
    )


def solution(mesh):
    return jax.shard_map(
        body,
        mesh=mesh,
        in_specs=(
            P(("patch", "head"), None),
            P(("patch", "head"), None),
            P(("patch", "head"), None),
            P(None, ("patch", "head")),
            P("patch", "head"),
            P("patch", "head"),
            P(None, "head"),
            P(None, "head"),
            P(None, "head"),
            P(),
        ),
        out_specs=(P(("patch", "head"), None), P(None, "head")),
        check_vma=False,
    )
```

```python
import functools

import jax
import jax.numpy as jnp
import numpy as np
from jax import lax
from jax.experimental import pallas as pl
from jax.experimental.pallas import tpu as pltpu
from jax.sharding import PartitionSpec as P

HD = 128
THETA = 256.0
MESH = pl.DeviceIdType.MESH
SCALE = 1.4426950408889634 * HD ** (-0.5)
LOW = -1e30
TILE = 1024
PIECE = 512
BLOCK = 128
TXT = 256

NEAR_A, NEAR_B, FAR, OWN = (4, 6, 8, 10), (5, 7, 9, 11), (12, 13, 14, 15), (0, 1, 2, 3)
ITEMS = [
    (0, NEAR_A), (1, NEAR_A),
    (2, OWN), (3, OWN),
    (2, NEAR_A), (3, NEAR_A),
    (2, NEAR_B), (3, NEAR_B),
    (2, FAR), (3, FAR),
    (0, NEAR_B), (0, FAR),
    (1, NEAR_B), (1, FAR),
]
ORDER16 = [1, 9, 2, 10, 3, 11, 4, 12, 5, 13, 6, 14, 7, 15, 8]
ORDER8 = [4, 1, 5, 2, 6, 3, 7, 0]


def rotation_tables():
    first = HD // 8
    second = (HD - first) // 2
    freqs = np.zeros((3, HD), np.float32)
    swap = np.zeros((HD, HD), np.float32)
    begin = 0
    for axis_id, width in enumerate([first, second, HD - first - second]):
        half = width // 2
        for index in range(half):
            low, high = begin + index, begin + index + half
            freqs[axis_id, low] = freqs[axis_id, high] = np.float32(THETA ** (-2.0 * index / width))
            swap[high, low] = -1.0
            swap[low, high] = 1.0
        begin += width
    terms = []
    for _ in range(3):
        term = freqs.astype(jnp.bfloat16)
        terms.append(term)
        freqs = freqs - term.astype(np.float32)
    return np.concatenate(terms + [np.zeros((7, HD), jnp.bfloat16)], axis=0), swap


def pick(i, values):
    out = values[0]
    for j in range(1, len(values)):
        if values[j] != values[j - 1]:
            out = jnp.where(i >= j, values[j], out)
    return out


def split_scaled(x):
    f = x.astype(jnp.float32) * SCALE
    hi = f.astype(jnp.bfloat16)
    lo = (f - hi.astype(jnp.float32)).astype(jnp.bfloat16)
    return jnp.concatenate([hi, lo], axis=1)


def scores(qq, k):
    return lax.dot_general(
        qq, jnp.concatenate([k, k], axis=1), (((1,), (1,)), ((), ())), preferred_element_type=jnp.float32
    )


def fold(s, v, m, a):
    top = jnp.maximum(m, jnp.max(s, axis=1, keepdims=True))
    p = jnp.exp2(s - top).astype(jnp.bfloat16)
    vv = jnp.concatenate([v, jnp.ones_like(v)], axis=1)
    a = a * jnp.exp2(m - top) + jnp.dot(p, vv, preferred_element_type=jnp.float32)
    return top, a


def kernel(
    q_in, k_in, v_in, pos_ref, freq_ref, swap_ref, sk_ref, sv_ref, tq_ref, tk_ref, tv_ref, len_ref,
    out_ref, tout_ref,
    q_ref, k_ref, v_ref, qh, kvh, qb, qq_s, kv, m_s, acc_s, o_send, l_send, o_recv, l_recv, out_stage, t_send, t_recv, t_stage,
    in_sem, q_sem, kv_sem, near_sem, core_sem, far_sem, y_sem, o_sem, out_sem, t_sem, tg_sem,
):
    p = lax.axis_index("patch")
    h = lax.axis_index("head")
    x, y, c = p // 4, (p // 2) % 2, p % 2
    me = h * 2 + c
    rank = x * 2 + y

    def at(x_, y_, c_):
        return (x_ * 4 + y_ * 2 + c_, h)

    left, right = (x + 3) % 4, (x + 1) % 4
    lanes = pl.ds(pl.multiple_of(c * HD, HD), HD)

    barrier = pltpu.get_barrier_semaphore()

    for d in range(1, 16):
        to = (me + d) % 16
        pl.semaphore_signal(barrier, inc=1, device_id=(x * 4 + y * 2 + to % 2, to // 2), device_id_type=MESH)
        pl.semaphore_signal(barrier, inc=1, device_id=((p + d) % 16, h), device_id_type=MESH)

    loads = [pltpu.make_async_copy(a, b, in_sem.at[n]) for n, (a, b) in enumerate(((q_in, q_ref), (k_in, k_ref), (v_in, v_ref)))]
    for half in range(2):
        for part in range(2):
            src = (sk_ref, sv_ref)[part].at[pl.ds(half * PIECE, PIECE), lanes]
            loads.append(pltpu.make_async_copy(src, kv.at[2 * c + half, part], in_sem.at[3 + 2 * half + part]))
    for load in loads:
        load.start()

    def remote(src, dst, sems, index, to):
        return pltpu.make_async_remote_copy(
            src_ref=src, dst_ref=dst, send_sem=sems.at[(0,) + index], recv_sem=sems.at[(1,) + index],
            device_id=to, device_id_type=MESH,
        )

    def whole(ref, sems, index=()):
        return remote(ref, ref, sems, index, at(x, y, 1 - c))

    def near(half, side, core, part):
        src = (sk_ref, sv_ref)[part].at[pl.ds(half * PIECE, PIECE), pl.ds(core * HD, HD)]
        piece = 4 + 4 * side + 2 * c + half
        return remote(src, kv.at[piece, part], near_sem, (half,), at((right, left)[side], y, core))

    def near_each(half, fn):
        for side in range(2):
            for part in range(2):
                for core in range(2):
                    fn(half, side, core, part)

    other = pl.ds(pl.multiple_of((1 - c) * HD, HD), HD)

    def across(half, part):
        src = (sk_ref, sv_ref)[part].at[pl.ds(half * PIECE, PIECE), other]
        return remote(src, kv.at[2 * c + half, part], core_sem, (), at(x, y, 1 - c))

    swap = swap_ref[...]
    pos = pos_ref[...].astype(jnp.float32)
    pos = jnp.concatenate([pos, pos, pos, jnp.zeros((7, BLOCK), jnp.float32)], axis=0).astype(jnp.bfloat16)
    angle = lax.dot_general(pos, freq_ref[...], (((0,), (0,)), ((), ())), preferred_element_type=jnp.float32)
    cosine, sine = jnp.cos(angle), jnp.sin(angle)

    def rotated(ref, g):
        value = ref[:, g * HD : (g + 1) * HD]
        turned = jnp.dot(value, swap, preferred_element_type=jnp.float32)
        return (value.astype(jnp.float32) * cosine + turned * sine).astype(jnp.bfloat16)

    def q_copy(d):
        to = (me + d) % 16
        return remote(qh.at[to], qb.at[c, h], q_sem, (), (x * 4 + y * 2 + to % 2, to // 2))

    def fresh_at(core, head):
        return kv.at[16 + 2 * core + head // 4, :, pl.ds(pl.multiple_of((head % 4) * BLOCK, BLOCK), BLOCK), :]

    def kv_copy(d):
        to = (me + d) % 16
        return remote(kvh.at[to], fresh_at(c, h), kv_sem, (), (x * 4 + y * 2 + to % 2, to // 2))

    def loop(low, high, fn):
        def step(d, _):
            fn(d)
            return 0

        lax.fori_loop(low, high, step, 0)

    loads[0].wait()
    for g in range(16):
        qh[g] = rotated(q_ref, g)
    loads[1].wait()
    loads[2].wait()
    for g in range(16):
        kvh[g, 0] = rotated(k_ref, g)
        kvh[g, 1] = v_ref[:, g * HD : (g + 1) * HD]

    for load in loads[3:]:
        load.wait()
    pl.semaphore_wait(barrier, 30)
    for d in ORDER16:
        q_copy(d).start()
    near_each(0, lambda *a: near(*a).start())
    for half in range(2):
        for part in range(2):
            across(half, part).start()
    for d in ORDER16:
        kv_copy(d).start()
    near_each(1, lambda *a: near(*a).start())

    qb[c, h] = qh[me]
    row = pl.multiple_of((h % 4) * BLOCK, BLOCK)
    kv[16 + 2 * c + h // 4, :, pl.ds(row, BLOCK), :] = kvh[me]

    def clear(t):
        m_s[t] = jnp.full((TILE, HD), LOW, jnp.float32)
        acc_s[t] = jnp.zeros((TILE, 2 * HD), jnp.float32)

    loop(0, 4, clear)

    def ready(t):
        qq_s[t] = split_scaled(qb[t].reshape(TILE, HD))

    def y_copy(t):
        return remote(qb.at[t], qb.at[2 + t], y_sem, (), at(x, 1 - y, c))

    whole(qh.at[pl.ds(0, 15)], q_sem).wait_recv()
    for t in range(2):
        y_copy(t).start()
    loop(0, 2, ready)

    def far(half, core, part):
        src = kv.at[4 + 4 * part + 2 * core + half, part]
        dst = kv.at[12 + 2 * core + half, part]
        return remote(src, dst, far_sem, (), at((right, left)[part], y, c))

    def near_ready(half):
        whole(kv.at[pl.ds(4, 4)], near_sem, (half,)).wait_recv()
        for core in range(2):
            for part in range(2):
                far(half, core, part).start()

    valid = lax.broadcasted_iota(jnp.int32, (1, TXT), 1) < len_ref[0]

    def attend(t, ids, text=False):
        qq = qq_s[t]
        m = jnp.max(m_s[t], axis=1, keepdims=True)
        a = acc_s[t]
        keys = [lambda n=n: scores(qq, kv[ids[n], 0]) for n in range(len(ids))]
        values = [lambda n=n: kv[ids[n], 1] for n in range(len(ids))]
        if text:
            keys.append(lambda: jnp.where(valid, scores(qq, tk_ref[:, lanes]), LOW))
            values.append(lambda: tv_ref[:, lanes])
        s = keys[0]()
        for n in range(len(keys)):
            following = keys[n + 1]() if n + 1 < len(keys) else None
            m, a = fold(s, values[n](), m, a)
            s = following
        m_s[t] = jnp.broadcast_to(m, (TILE, HD))
        acc_s[t] = a

    def text_copy(d):
        to = (rank + d) % 8
        src = t_send.at[:, pl.ds(pl.multiple_of(to * 32, 32), 32), :]
        return remote(src, t_recv.at[rank], t_sem, (), at(to // 2, to % 2, c))

    def text_queries():
        qq = split_scaled(tq_ref[:, lanes])
        m = jnp.full((TXT, 1), LOW, jnp.float32)
        a = jnp.zeros((TXT, 2 * HD), jnp.float32)
        for piece in range(16, 20):
            m, a = fold(scores(qq, kv[piece, 0]), kv[piece, 1], m, a)
        here = valid & (rank == 0)
        s = jnp.where(here, scores(qq, tk_ref[:, lanes]), LOW)
        m, a = fold(s, tv_ref[:, lanes], m, a)
        total = a[:, HD:]
        t_send[0] = a[:, :HD] / total
        t_send[1] = m + jnp.log2(total)
        loop(1, 8, lambda d: text_copy(d).start())
        t_recv[rank] = t_send[:, pl.ds(pl.multiple_of(rank * 32, 32), 32), :]

    def gather_copy(d):
        to = (p + d) % 16
        dst = tout_ref.at[pl.ds(pl.multiple_of(rank * 32, 32), 32), lanes]
        return remote(t_stage, dst, tg_sem, (), (to, h))

    def text_merge():
        whole(t_recv.at[pl.ds(0, 7)], t_sem).wait_recv()
        top = t_recv[0, 1]
        for r in range(1, 8):
            top = jnp.maximum(top, t_recv[r, 1])
        total = jnp.zeros((32, HD), jnp.float32)
        mixed = jnp.zeros((32, HD), jnp.float32)
        for r in range(8):
            w = jnp.exp2(t_recv[r, 1] - top)
            total += w
            mixed += w * t_recv[r, 0]
        done = (mixed / total).astype(jnp.bfloat16)
        t_stage[...] = done
        loop(1, 16, lambda d: gather_copy(d).start())
        tout_ref[pl.ds(pl.multiple_of(rank * 32, 32), 32), lanes] = done

    eye = lax.broadcasted_iota(jnp.int32, (HD, HD), 0) == lax.broadcasted_iota(jnp.int32, (HD, HD), 1)

    def o_copy(t):
        return remote(o_send.at[t], o_recv.at[t], o_sem, (t, 0), at(x, 1 - y, c))

    def l_copy(t):
        return remote(l_send.at[t], l_recv.at[t], o_sem, (t, 1), at(x, 1 - y, c))

    def give(t):
        total = acc_s[t][:, HD:]
        o_send[t - 2] = (acc_s[t][:, :HD] / total).astype(jnp.bfloat16)
        level = m_s[t] + jnp.log2(total)
        rows = []
        for b in range(TILE // HD):
            rows.append(jnp.sum(jnp.where(eye, level[b * HD : (b + 1) * HD], 0.0), axis=0, keepdims=True))
        l_send[t - 2] = jnp.concatenate(rows, axis=0)
        o_copy(t - 2).start()
        l_copy(t - 2).start()

    def out_copy(t, d):
        to = (h + d) % 8
        cols = pl.ds(pl.multiple_of(me * HD, HD), HD)
        return remote(out_stage.at[t, to], out_ref.at[:, cols], out_sem, (), (x * 4 + y * 2 + t, to))

    def take(t):
        o_copy(t).wait_recv()
        l_copy(t).wait_recv()
        own = jnp.where(t == c, 0, 1)
        for d in ORDER8:
            b = (h + d) % 8
            rows = pl.ds(pl.multiple_of(b * HD, HD), HD)
            total = acc_s[t, rows, HD:]
            level = m_s[t, rows] + jnp.log2(total)
            lev = jnp.sum(jnp.where(eye, l_recv[t, pl.ds(b, 1)], 0.0), axis=1, keepdims=True)
            top = jnp.maximum(level, lev)
            wa, wb = jnp.exp2(level - top), jnp.exp2(lev - top)
            mixed = acc_s[t, rows, :HD] * (wa / total) + o_recv[t, rows].astype(jnp.float32) * wb
            out_stage[t, b] = (mixed / (wa + wb)).astype(jnp.bfloat16)
            if d != 0:
                out_copy(t, d).start()

        @pl.when(own != 0)
        def _():
            out_copy(t, 0).start()

        @pl.when(own == 0)
        def _():
            out_ref[:, pl.ds(pl.multiple_of(me * HD, HD), HD)] = out_stage[t, h]

    def item(i):
        @pl.when(i == 0)
        def _():
            near_ready(0)

        @pl.when(i == 2)
        def _():
            whole(kvh.at[pl.ds(0, 15)], kv_sem).wait_recv()
            loop(0, 2, lambda t: attend(t, (16 + 2 * t, 17 + 2 * t)))
            near_ready(1)
            text_queries()
            whole(qb.at[pl.ds(2, 2)], y_sem).wait_recv()
            loop(2, 4, ready)

        @pl.when(i == 5)
        def _():
            text_merge()

        @pl.when(i == 8)
        def _():
            whole(kv.at[pl.ds(12, 4)], far_sem).wait_recv()

        t = pick(i, [q for q, _ in ITEMS])
        ids = [pick(i, [pieces[n] for _, pieces in ITEMS]) for n in range(4)]
        attend(t, ids)

        @pl.when((i >= 8) & (i < 10))
        def _():
            give(t)

        @pl.when((i == 11) | (i == 13))
        def _():
            take(t)

    whole(kv.at[pl.ds(0, 2)], core_sem).wait_recv()
    loop(0, 2, lambda t: attend(t, (2 - 2 * t, 3 - 2 * t), text=True))
    loop(0, 14, item)

    for half in range(2):
        whole(kv.at[pl.ds(4, 4)], near_sem, (half,)).wait_send()
    whole(qh.at[pl.ds(0, 15)], q_sem).wait_send()
    whole(kvh.at[pl.ds(0, 15)], kv_sem).wait_send()
    whole(kv.at[pl.ds(0, 2)], core_sem).wait_send()
    whole(kv.at[pl.ds(12, 4)], far_sem).wait_send()
    whole(qb.at[pl.ds(2, 2)], y_sem).wait_send()
    for t in range(2):
        o_copy(t).wait_send()
        l_copy(t).wait_send()
    whole(t_recv.at[pl.ds(0, 7)], t_sem).wait_send()
    whole(qh.at[pl.ds(0, 15), pl.ds(0, 32)], tg_sem).wait_send()
    whole(qh.at[pl.ds(0, 15), pl.ds(0, 32)], tg_sem).wait_recv()
    whole(qh.at[pl.ds(0, 15)], out_sem).wait_send()
    whole(qh.at[pl.ds(0, 15)], out_sem).wait_recv()


def body(image_query, image_key, image_value, positions, stale_key, stale_value, text_query, text_key, text_value, text_len):
    freqs, swap = rotation_tables()
    dma = pltpu.SemaphoreType.DMA
    bf, f32 = jnp.bfloat16, jnp.float32
    vmem = pl.BlockSpec(memory_space=pltpu.VMEM)
    anywhere = pl.BlockSpec(memory_space=pl.ANY)
    return pl.pallas_call(
        kernel,
        out_shape=(
            jax.ShapeDtypeStruct(image_query.shape, bf),
            jax.ShapeDtypeStruct(text_query.shape, bf),
        ),
        in_specs=[anywhere] * 3 + [vmem] * 3 + [anywhere] * 2 + [vmem] * 3 + [pl.BlockSpec(memory_space=pltpu.SMEM)],
        out_specs=(vmem, vmem),
        scratch_shapes=[
            pltpu.VMEM(image_query.shape, bf),
            pltpu.VMEM(image_key.shape, bf),
            pltpu.VMEM(image_value.shape, bf),
            pltpu.VMEM((16, BLOCK, HD), bf),
            pltpu.VMEM((16, 2, BLOCK, HD), bf),
            pltpu.VMEM((4, 8, BLOCK, HD), bf),
            pltpu.VMEM((4, TILE, 2 * HD), bf),
            pltpu.VMEM((20, 2, PIECE, HD), bf),
            pltpu.VMEM((4, TILE, HD), f32),
            pltpu.VMEM((4, TILE, 2 * HD), f32),
            pltpu.VMEM((2, TILE, HD), bf),
            pltpu.VMEM((2, 8, HD), f32),
            pltpu.VMEM((2, TILE, HD), bf),
            pltpu.VMEM((2, 8, HD), f32),
            pltpu.VMEM((2, 8, BLOCK, HD), bf),
            pltpu.VMEM((2, TXT, HD), f32),
            pltpu.VMEM((8, 2, 32, HD), f32),
            pltpu.VMEM((32, HD), bf),
            dma((7,)),
            dma((2,)),
            dma((2,)),
            dma((2, 2)),
            dma((2,)),
            dma((2,)),
            dma((2,)),
            dma((2, 2, 2)),
            dma((2,)),
            dma((2,)),
            dma((2,)),
        ],
        compiler_params=pltpu.CompilerParams(
            collective_id=0, has_side_effects=True, vmem_limit_bytes=56 * 2**20
        ),
        name="joint_attention",
    )(
        image_query, image_key, image_value, positions, jnp.asarray(freqs), jnp.asarray(swap, bf),
        stale_key, stale_value, text_query, text_key, text_value, text_len,
    )


def solution(mesh):
    return jax.shard_map(
        body,
        mesh=mesh,
        in_specs=(
            P(("patch", "head"), None),
            P(("patch", "head"), None),
            P(("patch", "head"), None),
            P(None, ("patch", "head")),
            P("patch", "head"),
            P("patch", "head"),
            P(None, "head"),
            P(None, "head"),
            P(None, "head"),
            P(),
        ),
        out_specs=(P(("patch", "head"), None), P(None, "head")),
        check_vma=False,
    )
```

```python
import functools

import jax
import jax.numpy as jnp
import numpy as np
from jax import lax
from jax.experimental import pallas as pl
from jax.experimental.pallas import tpu as pltpu
from jax.sharding import PartitionSpec as P

HD = 128
THETA = 256.0
MESH = pl.DeviceIdType.MESH
SCALE = 1.4426950408889634 * HD ** (-0.5)
LOW = -1e30
TILE = 1024
PIECE = 512
BLOCK = 128
TXT = 256

NEAR_A, NEAR_B, FAR, OWN = (4, 6, 8, 10), (5, 7, 9, 11), (12, 13, 14, 15), (0, 1, 2, 3)
ITEMS = [
    (0, NEAR_A), (1, NEAR_A),
    (0, NEAR_B),
    (2, OWN), (2, NEAR_A), (2, NEAR_B), (2, FAR),
    (3, OWN), (3, NEAR_A), (3, NEAR_B), (3, FAR),
    (0, FAR), (1, NEAR_B),
]
ORDER16 = [1, 9, 2, 10, 3, 11, 4, 12, 5, 13, 6, 14, 7, 15, 8]
ORDER8 = [4, 1, 5, 2, 6, 3, 7, 0]


def rotation_tables():
    first = HD // 8
    second = (HD - first) // 2
    freqs = np.zeros((3, HD), np.float32)
    swap = np.zeros((HD, HD), np.float32)
    begin = 0
    for axis_id, width in enumerate([first, second, HD - first - second]):
        half = width // 2
        for index in range(half):
            low, high = begin + index, begin + index + half
            freqs[axis_id, low] = freqs[axis_id, high] = np.float32(THETA ** (-2.0 * index / width))
            swap[high, low] = -1.0
            swap[low, high] = 1.0
        begin += width
    terms = []
    for _ in range(3):
        term = freqs.astype(jnp.bfloat16)
        terms.append(term)
        freqs = freqs - term.astype(np.float32)
    return np.concatenate(terms + [np.zeros((7, HD), jnp.bfloat16)], axis=0), swap


def pick(i, values):
    out = values[0]
    for j in range(1, len(values)):
        if values[j] != values[j - 1]:
            out = jnp.where(i >= j, values[j], out)
    return out


def split_scaled(x):
    f = x.astype(jnp.float32) * SCALE
    hi = f.astype(jnp.bfloat16)
    lo = (f - hi.astype(jnp.float32)).astype(jnp.bfloat16)
    return jnp.concatenate([hi, lo], axis=1)


def scores(qq, k):
    return lax.dot_general(
        qq, jnp.concatenate([k, k], axis=1), (((1,), (1,)), ((), ())), preferred_element_type=jnp.float32
    )


def fold(s, v, m, a):
    top = jnp.maximum(m, jnp.max(s, axis=1, keepdims=True))
    p = jnp.exp2(s - top).astype(jnp.bfloat16)
    vv = jnp.concatenate([v, jnp.ones_like(v)], axis=1)
    a = a * jnp.exp2(m - top) + jnp.dot(p, vv, preferred_element_type=jnp.float32)
    return top, a


def kernel(
    q_in, k_in, v_in, pos_ref, freq_ref, swap_ref, sk_ref, sv_ref, tq_ref, tk_ref, tv_ref, len_ref,
    out_ref, tout_ref,
    q_ref, k_ref, v_ref, qh, kvh, qb, qq_s, kv, m_s, acc_s, o_send, l_send, o_recv, l_recv, out_stage, t_send, t_recv, t_stage,
    in_sem, q_sem, kv_sem, near_sem, core_sem, far_sem, y_sem, o_sem, out_sem, t_sem, tg_sem,
):
    p = lax.axis_index("patch")
    h = lax.axis_index("head")
    x, y, c = p // 4, (p // 2) % 2, p % 2
    me = h * 2 + c
    rank = x * 2 + y

    def at(x_, y_, c_):
        return (x_ * 4 + y_ * 2 + c_, h)

    left, right = (x + 3) % 4, (x + 1) % 4
    lanes = pl.ds(pl.multiple_of(c * HD, HD), HD)

    barrier = pltpu.get_barrier_semaphore()

    for d in range(1, 16):
        to = (me + d) % 16
        pl.semaphore_signal(barrier, inc=1, device_id=(x * 4 + y * 2 + to % 2, to // 2), device_id_type=MESH)
        pl.semaphore_signal(barrier, inc=1, device_id=((p + d) % 16, h), device_id_type=MESH)

    loads = [pltpu.make_async_copy(a, b, in_sem.at[n]) for n, (a, b) in enumerate(((q_in, q_ref), (k_in, k_ref), (v_in, v_ref)))]
    for half in range(2):
        for part in range(2):
            src = (sk_ref, sv_ref)[part].at[pl.ds(half * PIECE, PIECE), lanes]
            loads.append(pltpu.make_async_copy(src, kv.at[2 * c + half, part], in_sem.at[3 + 2 * half + part]))
    for load in loads:
        load.start()

    def remote(src, dst, sems, index, to):
        return pltpu.make_async_remote_copy(
            src_ref=src, dst_ref=dst, send_sem=sems.at[(0,) + index], recv_sem=sems.at[(1,) + index],
            device_id=to, device_id_type=MESH,
        )

    def whole(ref, sems, index=()):
        return remote(ref, ref, sems, index, at(x, y, 1 - c))

    def near(half, side, core, part):
        src = (sk_ref, sv_ref)[part].at[pl.ds(half * PIECE, PIECE), pl.ds(core * HD, HD)]
        piece = 4 + 4 * side + 2 * c + half
        return remote(src, kv.at[piece, part], near_sem, (half,), at((right, left)[side], y, core))

    def near_each(half, fn):
        for side in range(2):
            for part in range(2):
                for core in range(2):
                    fn(half, side, core, part)

    other = pl.ds(pl.multiple_of((1 - c) * HD, HD), HD)

    def across(half, part):
        src = (sk_ref, sv_ref)[part].at[pl.ds(half * PIECE, PIECE), other]
        return remote(src, kv.at[2 * c + half, part], core_sem, (), at(x, y, 1 - c))

    swap = swap_ref[...]
    pos = pos_ref[...].astype(jnp.float32)
    pos = jnp.concatenate([pos, pos, pos, jnp.zeros((7, BLOCK), jnp.float32)], axis=0).astype(jnp.bfloat16)
    angle = lax.dot_general(pos, freq_ref[...], (((0,), (0,)), ((), ())), preferred_element_type=jnp.float32)
    cosine, sine = jnp.cos(angle), jnp.sin(angle)

    def rotated(ref, g):
        value = ref[:, g * HD : (g + 1) * HD]
        turned = jnp.dot(value, swap, preferred_element_type=jnp.float32)
        return (value.astype(jnp.float32) * cosine + turned * sine).astype(jnp.bfloat16)

    def q_copy(d):
        to = (me + d) % 16
        return remote(qh.at[to], qb.at[c, h], q_sem, (c,), (x * 4 + y * 2 + to % 2, to // 2))

    def fresh_at(core, head):
        return kv.at[16 + 2 * core + head // 4, :, pl.ds(pl.multiple_of((head % 4) * BLOCK, BLOCK), BLOCK), :]

    def kv_copy(d):
        to = (me + d) % 16
        return remote(kvh.at[to], fresh_at(c, h), kv_sem, (), (x * 4 + y * 2 + to % 2, to // 2))

    def loop(low, high, fn):
        def step(d, _):
            fn(d)
            return 0

        lax.fori_loop(low, high, step, 0)

    loads[0].wait()
    for g in range(16):
        qh[g] = rotated(q_ref, g)
    loads[1].wait()
    loads[2].wait()
    for g in range(16):
        kvh[g, 0] = rotated(k_ref, g)
        kvh[g, 1] = v_ref[:, g * HD : (g + 1) * HD]

    for load in loads[3:]:
        load.wait()
    pl.semaphore_wait(barrier, 30)

    def send_queries():
        for d in ORDER16:
            q_copy(d).start()

    pl.when(c == 0)(send_queries)
    for half in range(2):
        for part in range(2):
            across(half, part).start()
    pl.when(c == 1)(send_queries)
    for d in ORDER16:
        kv_copy(d).start()
    near_each(0, lambda *a: near(*a).start())
    near_each(1, lambda *a: near(*a).start())

    qb[c, h] = qh[me]
    row = pl.multiple_of((h % 4) * BLOCK, BLOCK)
    kv[16 + 2 * c + h // 4, :, pl.ds(row, BLOCK), :] = kvh[me]

    def clear(t):
        m_s[t] = jnp.full((TILE, HD), LOW, jnp.float32)
        acc_s[t] = jnp.zeros((TILE, 2 * HD), jnp.float32)

    loop(0, 4, clear)

    def ready(t):
        qq_s[t] = split_scaled(qb[t].reshape(TILE, HD))

    def y_copy(t):
        return remote(qb.at[t], qb.at[2 + t], y_sem, (), at(x, 1 - y, c))


    def far(half, core, part):
        src = kv.at[4 + 4 * part + 2 * core + half, part]
        dst = kv.at[12 + 2 * core + half, part]
        return remote(src, dst, far_sem, (), at((right, left)[part], y, c))

    def near_ready(half):
        whole(kv.at[pl.ds(4, 4)], near_sem, (half,)).wait_recv()
        for core in range(2):
            for part in range(2):
                far(half, core, part).start()

    valid = lax.broadcasted_iota(jnp.int32, (1, TXT), 1) < len_ref[0]

    def attend(t, ids, text=False, rows=pl.ds(0, TILE)):
        qq = qq_s[t, rows]
        m = jnp.max(m_s[t, rows], axis=1, keepdims=True)
        a = acc_s[t, rows]
        keys = [lambda n=n: scores(qq, kv[ids[n], 0]) for n in range(len(ids))]
        values = [lambda n=n: kv[ids[n], 1] for n in range(len(ids))]
        if text:
            keys.append(lambda: jnp.where(valid, scores(qq, tk_ref[:, lanes]), LOW))
            values.append(lambda: tv_ref[:, lanes])
        s = keys[0]()
        for n in range(len(keys)):
            following = keys[n + 1]() if n + 1 < len(keys) else None
            m, a = fold(s, values[n](), m, a)
            s = following
        m_s[t, rows] = jnp.broadcast_to(m, (a.shape[0], HD))
        acc_s[t, rows] = a

    def text_copy(d):
        to = (rank + d) % 8
        src = t_send.at[:, pl.ds(pl.multiple_of(to * 32, 32), 32), :]
        return remote(src, t_recv.at[rank], t_sem, (), at(to // 2, to % 2, c))

    def text_queries():
        qq = split_scaled(tq_ref[:, lanes])
        m = jnp.full((TXT, 1), LOW, jnp.float32)
        a = jnp.zeros((TXT, 2 * HD), jnp.float32)
        for piece in range(16, 20):
            m, a = fold(scores(qq, kv[piece, 0]), kv[piece, 1], m, a)
        here = valid & (rank == 0)
        s = jnp.where(here, scores(qq, tk_ref[:, lanes]), LOW)
        m, a = fold(s, tv_ref[:, lanes], m, a)
        total = a[:, HD:]
        t_send[0] = a[:, :HD] / total
        t_send[1] = m + jnp.log2(total)
        loop(1, 8, lambda d: text_copy(d).start())
        t_recv[rank] = t_send[:, pl.ds(pl.multiple_of(rank * 32, 32), 32), :]

    def gather_copy(d):
        to = (p + d) % 16
        dst = tout_ref.at[pl.ds(pl.multiple_of(rank * 32, 32), 32), lanes]
        return remote(t_stage, dst, tg_sem, (), (to, h))

    def text_own():
        return pltpu.make_async_copy(t_stage, tout_ref.at[pl.ds(pl.multiple_of(rank * 32, 32), 32), lanes], in_sem.at[8])

    def text_merge():
        whole(t_recv.at[pl.ds(0, 7)], t_sem).wait_recv()
        top = t_recv[0, 1]
        for r in range(1, 8):
            top = jnp.maximum(top, t_recv[r, 1])
        total = jnp.zeros((32, HD), jnp.float32)
        mixed = jnp.zeros((32, HD), jnp.float32)
        for r in range(8):
            w = jnp.exp2(t_recv[r, 1] - top)
            total += w
            mixed += w * t_recv[r, 0]
        done = (mixed / total).astype(jnp.bfloat16)
        t_stage[...] = done
        loop(1, 16, lambda d: gather_copy(d).start())
        text_own().start()

    eye = lax.broadcasted_iota(jnp.int32, (HD, HD), 0) == lax.broadcasted_iota(jnp.int32, (HD, HD), 1)

    def o_copy(t):
        return remote(o_send.at[t], o_recv.at[t], o_sem, (t, 0), at(x, 1 - y, c))

    def l_copy(t):
        return remote(l_send.at[t], l_recv.at[t], o_sem, (t, 1), at(x, 1 - y, c))

    def give(t):
        total = acc_s[t][:, HD:]
        o_send[t - 2] = (acc_s[t][:, :HD] / total).astype(jnp.bfloat16)
        level = m_s[t] + jnp.log2(total)
        rows = []
        for b in range(TILE // HD):
            rows.append(jnp.sum(jnp.where(eye, level[b * HD : (b + 1) * HD], 0.0), axis=0, keepdims=True))
        l_send[t - 2] = jnp.concatenate(rows, axis=0)
        o_copy(t - 2).start()
        l_copy(t - 2).start()

    mine = pl.ds(pl.multiple_of(me * HD, HD), HD)

    def out_copy(t, b):
        return remote(out_stage.at[t, b], out_ref.at[:, mine], out_sem, (), (x * 4 + y * 2 + t, b))

    def own_copy():
        return pltpu.make_async_copy(out_stage.at[c, h], out_ref.at[:, mine], in_sem.at[7])

    def take(t, b):
        rows = pl.ds(pl.multiple_of(b * HD, HD), HD)
        total = acc_s[t, rows, HD:]
        level = m_s[t, rows] + jnp.log2(total)
        lev = jnp.sum(jnp.where(eye, l_recv[t, pl.ds(b, 1)], 0.0), axis=1, keepdims=True)
        top = jnp.maximum(level, lev)
        wa, wb = jnp.exp2(level - top), jnp.exp2(lev - top)
        mixed = acc_s[t, rows, :HD] * (wa / total) + o_recv[t, rows].astype(jnp.float32) * wb
        out_stage[t, b] = (mixed / (wa + wb)).astype(jnp.bfloat16)

        @pl.when((t != c) | (b != h))
        def _():
            out_copy(t, b).start()

        @pl.when((t == c) & (b == h))
        def _():
            own_copy().start()

    def item(i):
        @pl.when(i == 0)
        def _():
            near_ready(0)

        @pl.when(i == 2)
        def _():
            whole(kvh.at[pl.ds(0, 15)], kv_sem).wait_recv()
            loop(0, 2, lambda t: attend(t, (16 + 2 * t, 17 + 2 * t)))
            near_ready(1)
            text_queries()

        @pl.when(i == 3)
        def _():
            whole(qb.at[pl.ds(2, 2)], y_sem).wait_recv()
            loop(2, 4, ready)

        @pl.when(i == 6)
        def _():
            text_merge()
            whole(kv.at[pl.ds(12, 4)], far_sem).wait_recv()

        t = pick(i, [q for q, _ in ITEMS])
        ids = [pick(i, [pieces[n] for _, pieces in ITEMS]) for n in range(4)]
        attend(t, ids)

        @pl.when((i == 6) | (i == 10))
        def _():
            give(t)

        @pl.when(i == 11)
        def _():
            o_copy(0).wait_recv()
            l_copy(0).wait_recv()
            for d in ORDER8:
                take(0, (h + d) % 8)

    def begin(t):
        @pl.when(t == c)
        def _():
            whole(qh.at[pl.ds(0, 7)], q_sem, (t,)).wait_recv()

        @pl.when(t != c)
        def _():
            whole(qh.at[pl.ds(0, 8)], q_sem, (t,)).wait_recv()

        y_copy(t).start()
        ready(t)
        attend(t, (2 - 2 * t, 3 - 2 * t), text=True)

    def finish(half):
        side = (h // 4 + 1 + half) % 2
        attend(1, FAR, rows=pl.ds(pl.multiple_of(side * PIECE, PIECE), PIECE))

        @pl.when(half == 0)
        def _():
            o_copy(1).wait_recv()
            l_copy(1).wait_recv()

        for d in (1, 2, 3, 0):
            take(1, side * 4 + (h + d) % 4)

    whole(kv.at[pl.ds(0, 2)], core_sem).wait_recv()
    loop(0, 2, begin)
    loop(0, 13, item)
    loop(0, 2, finish)

    for half in range(2):
        whole(kv.at[pl.ds(4, 4)], near_sem, (half,)).wait_send()
    whole(qh.at[pl.ds(0, 15)], q_sem, (c,)).wait_send()
    whole(kvh.at[pl.ds(0, 15)], kv_sem).wait_send()
    whole(kv.at[pl.ds(0, 2)], core_sem).wait_send()
    whole(kv.at[pl.ds(12, 4)], far_sem).wait_send()
    whole(qb.at[pl.ds(2, 2)], y_sem).wait_send()
    for t in range(2):
        o_copy(t).wait_send()
        l_copy(t).wait_send()
    whole(t_recv.at[pl.ds(0, 7)], t_sem).wait_send()
    whole(qh.at[pl.ds(0, 15), pl.ds(0, 32)], tg_sem).wait_send()
    whole(qh.at[pl.ds(0, 15), pl.ds(0, 32)], tg_sem).wait_recv()
    text_own().wait()
    own_copy().wait()
    whole(qh.at[pl.ds(0, 15)], out_sem).wait_send()
    whole(qh.at[pl.ds(0, 15)], out_sem).wait_recv()


def body(image_query, image_key, image_value, positions, stale_key, stale_value, text_query, text_key, text_value, text_len):
    freqs, swap = rotation_tables()
    dma = pltpu.SemaphoreType.DMA
    bf, f32 = jnp.bfloat16, jnp.float32
    vmem = pl.BlockSpec(memory_space=pltpu.VMEM)
    anywhere = pl.BlockSpec(memory_space=pl.ANY)
    return pl.pallas_call(
        kernel,
        out_shape=(
            jax.ShapeDtypeStruct(image_query.shape, bf),
            jax.ShapeDtypeStruct(text_query.shape, bf),
        ),
        in_specs=[anywhere] * 3 + [vmem] * 3 + [anywhere] * 2 + [vmem] * 3 + [pl.BlockSpec(memory_space=pltpu.SMEM)],
        out_specs=(anywhere, anywhere),
        scratch_shapes=[
            pltpu.VMEM(image_query.shape, bf),
            pltpu.VMEM(image_key.shape, bf),
            pltpu.VMEM(image_value.shape, bf),
            pltpu.VMEM((16, BLOCK, HD), bf),
            pltpu.VMEM((16, 2, BLOCK, HD), bf),
            pltpu.VMEM((4, 8, BLOCK, HD), bf),
            pltpu.VMEM((4, TILE, 2 * HD), bf),
            pltpu.VMEM((20, 2, PIECE, HD), bf),
            pltpu.VMEM((4, TILE, HD), f32),
            pltpu.VMEM((4, TILE, 2 * HD), f32),
            pltpu.VMEM((2, TILE, HD), bf),
            pltpu.VMEM((2, 8, HD), f32),
            pltpu.VMEM((2, TILE, HD), bf),
            pltpu.VMEM((2, 8, HD), f32),
            pltpu.VMEM((2, 8, BLOCK, HD), bf),
            pltpu.VMEM((2, TXT, HD), f32),
            pltpu.VMEM((8, 2, 32, HD), f32),
            pltpu.VMEM((32, HD), bf),
            dma((9,)),
            dma((2, 2)),
            dma((2,)),
            dma((2, 2)),
            dma((2,)),
            dma((2,)),
            dma((2,)),
            dma((2, 2, 2)),
            dma((2,)),
            dma((2,)),
            dma((2,)),
        ],
        compiler_params=pltpu.CompilerParams(
            collective_id=0, has_side_effects=True, vmem_limit_bytes=56 * 2**20
        ),
        name="joint_attention",
    )(
        image_query, image_key, image_value, positions, jnp.asarray(freqs), jnp.asarray(swap, bf),
        stale_key, stale_value, text_query, text_key, text_value, text_len,
    )


def solution(mesh):
    return jax.shard_map(
        body,
        mesh=mesh,
        in_specs=(
            P(("patch", "head"), None),
            P(("patch", "head"), None),
            P(("patch", "head"), None),
            P(None, ("patch", "head")),
            P("patch", "head"),
            P("patch", "head"),
            P(None, "head"),
            P(None, "head"),
            P(None, "head"),
            P(),
        ),
        out_specs=(P(("patch", "head"), None), P(None, "head")),
        check_vma=False,
    )
```
